32 devices in a mesh: expert: 4 (over z), tensor: 8 (over y, x, core).
Axes of the slice: x: 2, y: 2, z: 4, core: 2. Of those that a mesh axis runs over, the one named last changes fastest.
Arguments:
- tokens: bfloat16 [512, 5120], P('expert', 'tensor'), may hold values from -6 to 6
- routes: int32 [512, 6], P('expert'), may hold values from 0 to 15, all different within a row; in each aligned block of 128 rows (0 to 127, 128 to 255, ...) at most 64 rows name the same one
- gates: float32 [512, 6], P('expert'), may hold values from 0.05 to 0.35
- w_gate: bfloat16 [16, 1536, 5120], P('expert', 'tensor'), may hold values from -0.078125 to 0.078125
- w_up: bfloat16 [16, 1536, 5120], P('expert', 'tensor'), may hold values from -0.078125 to 0.078125
- w_down: bfloat16 [16, 1536, 5120], P('expert', None, 'tensor'), may hold values from -0.15625 to 0.15625
- shared_gate: bfloat16 [1536, 5120], P('tensor'), may hold values from -0.078125 to 0.078125
- shared_up: bfloat16 [1536, 5120], P('tensor'), may hold values from -0.078125 to 0.078125
- shared_down: bfloat16 [1536, 5120], P(None, 'tensor'), may hold values from -0.15625 to 0.15625
- vocab: bfloat16 [4096, 5120], P(('expert', 'tensor'))
- targets: int32 [16], replicated, may hold values from 0 to 4095
Outputs:
- layer_out: bfloat16 [512, 5120], P('expert', 'tensor')
- loglik: float32 [16], replicated
The draws below stay inside these ranges and needn't reach their ends.
Inputs may be any that keep to these rules, and one draw needn't show every extreme that they name: `routes`: the tokens of one group name one expert at most 64 times; in every draw some group names some expert exactly 64 times.
All inputs are finite; a program needn't handle non-finite values.
Results may differ from the reference program's by a relative error of at most 0.0041.
Values may be sent and summed in bfloat16 or wider, within the bound.
A program may use at most 128 MiB of HBM per device.

```python
import math
import jax
import jax.numpy as jnp
import numpy as np
from jax import lax

D = 5120
FF = 1536
TOPK = 6
EXPERTS = 16
TOK_E = 128
SCORE_E = 4
CAP = 64
TOKENS = 512
SCORED = 16
V = 4096
N_EXPERT = 4


def draw_vocab(key, part):
    first, second = jax.random.split(key)
    position = jnp.arange(V, dtype=jnp.float32)[:, None] / V
    spread = jnp.exp(jax.random.uniform(second, (V, 1), jnp.float32, 0.0, math.log(3.0)))
    base = jax.random.normal(first, (V, D), jnp.float32)
    scale = 1.1 * spread * (1.0 + 0.6 * position)
    return (base * scale / math.sqrt(D)).astype(jnp.bfloat16)


def with_ends(values, rng, smallest, high):
    dims = values.shape
    spot = [jax.random.randint(jax.random.fold_in(rng, axis), (), 0, dims[axis]) for axis in range(len(dims))]
    values = values.at[tuple(spot)].set(smallest)
    longest = dims.index(max(dims))
    spot[longest] = (spot[longest] + 1) % dims[longest]
    return values.at[tuple(spot)].set(high)


def level_of(key, dims, cuts, low, high):
    def one(axis_at, blocks):
        heights = jax.random.uniform(jax.random.fold_in(jax.random.fold_in(key, 6), axis_at), (blocks,), jnp.float32, low / len(cuts), high / len(cuts))
        return jnp.repeat(jnp.exp(heights), dims[axis_at] // blocks).reshape((-1,) + (1,) * (len(dims) - axis_at - 1))

    loudness = one(*cuts[0])
    for cut in cuts[1:]:
        loudness = loudness * one(*cut)
    return loudness


def routed_block(rng, own, number, rows, number_of, top, limit, lean):
    sequence = jax.random.permutation(rng, number_of)
    heavy_load, common = shares(number_of, rows * top, limit, lean, True), shares(number_of, rows * top, limit, lean, False)
    places = jnp.arange(number_of)

    def named(lengths, offset_by):
        used = int((lengths > 0).sum())
        fixed = max(1, used // 4)
        moved = fixed + (places - fixed + offset_by * (used - fixed)) % max(1, number_of - fixed)
        return jnp.zeros((number_of,), jnp.int32).at[sequence[jnp.where(places < fixed, places, moved)]].set(jnp.asarray(lengths, jnp.int32))

    lengths = jnp.where(number % 4 == 0, named(heavy_load, number // 4), named(common, number - number // 4 - 1))
    mixed = jax.random.permutation(jax.random.fold_in(own, 3), number_of)
    source_of, receiver = mixed[0:number_of // 2 * 2:2], mixed[1:number_of // 2 * 2:2]
    slack = jnp.minimum(lengths[source_of] - 1, limit - lengths[receiver]) // 2
    slack = jnp.where((source_of == sequence[0]) | (receiver == sequence[0]) | (lengths[receiver] == 0), 0, jnp.maximum(slack, 0))
    moved = jax.random.randint(jax.random.fold_in(own, 4), (number_of // 2,), 0, 1 << 20) % (slack + 1)
    lengths = lengths.at[source_of].add(-moved).at[receiver].add(moved)
    labels = jnp.searchsorted(jnp.cumsum(lengths), jnp.arange(rows * top), side="right").astype(jnp.int32)
    table = labels.reshape(top, rows).T
    table = table[jax.random.permutation(jax.random.fold_in(own, 1), rows)]
    offset_by = jax.random.randint(jax.random.fold_in(own, 2), (rows, 1), 0, top)
    return jnp.take_along_axis(table, (jnp.arange(top)[None, :] + offset_by) % top, axis=1)


def shares(amount, total, reach, lean, full):
    weights = [(1 << 20) // math.isqrt(rank ** lean) + 1 for rank in range(1, amount + 1)]
    largest = reach if full else min(reach, max(-(-total // amount), total * weights[0] // sum(weights)))
    least = 1 if total - largest >= amount - 1 else 0
    counts, rest = [largest] + [least] * (amount - 1), total - largest - least * (amount - 1)
    while rest > 0:
        candidates = [i for i in range(1, amount) if counts[i] < largest] or [i for i in range(1, amount) if counts[i] < reach]
        mass, left = sum([weights[i] for i in candidates]), rest
        for i in candidates:
            addition = min(reach - counts[i], max(1, left * weights[i] // mass), rest)
            counts[i] = counts[i] + addition
            rest = rest - addition
    return np.array(counts)


def centred(stream_key, extent, width, reach, shards=(), kind=jnp.bfloat16):
    values = width * jax.random.normal(stream_key, extent, jnp.float32)
    if shards:
        values = values * level_of(stream_key, extent, shards, -0.22, 0.18)
    return jnp.clip(values, -reach, reach).astype(kind)


def setup_inputs(seed: int = 0) -> dict:
    keys = jax.random.split(jax.random.key(seed), 12)
    tokens = centred(keys[0], (TOKENS, D), 1.0, 6.0, ((0, 4), (1, 8)))
    routes_keys = jax.random.split(jax.random.fold_in(keys[1], 1), TOKENS // TOK_E)
    routes_turns = jax.random.permutation(jax.random.fold_in(keys[1], 3), TOKENS // TOK_E)
    routes = jax.vmap(lambda own, number: routed_block(jax.random.fold_in(keys[1], 2), own, number, TOK_E, EXPERTS, TOPK, CAP, 2))(routes_keys, routes_turns).reshape((TOKENS, TOPK))
    gates = jnp.clip(0.05 + 0.29999999 * jax.random.uniform(keys[2], (TOKENS, TOPK), jnp.float32) ** level_of(keys[2], (TOKENS, TOPK), ((0, 4),), -0.2, 0.2), 0.05, 0.35)
    w_gate = centred(keys[3], (EXPERTS, FF, D), D ** -0.5, 0.078125, ((0, 4), (1, 8)))
    w_up = centred(keys[4], (EXPERTS, FF, D), D ** -0.5, 0.078125, ((0, 4), (1, 8)))
    w_down = centred(keys[5], (EXPERTS, FF, D), FF ** -0.5, 0.15625, ((0, 4), (2, 8)))
    shared_gate = centred(keys[6], (FF, D), D ** -0.5, 0.078125, ((0, 8),))
    shared_up = centred(keys[7], (FF, D), D ** -0.5, 0.078125, ((0, 8),))
    shared_down = centred(keys[8], (FF, D), FF ** -0.5, 0.15625, ((1, 8),))
    vocab = draw_vocab(jax.random.fold_in(keys[11], 71), 0)
    targets = with_ends(jax.random.randint(keys[10], (SCORED,), 0, V), jax.random.fold_in(keys[10], 1), 0, V - 1).astype(jnp.int32)
    return {"tokens": tokens, "routes": routes, "gates": gates, "w_gate": w_gate, "w_up": w_up, "w_down": w_down, "shared_gate": shared_gate, "shared_up": shared_up, "shared_down": shared_down, "vocab": vocab, "targets": targets}


def slot_tables(routes, gates):
    picks = (routes[:, :, None] == jnp.arange(EXPERTS, dtype=jnp.int32)[None, None, :]).astype(jnp.int32)
    per_token = jnp.sum(picks, axis=1)
    earlier = jnp.cumsum(per_token, axis=0) - per_token
    slots = jnp.sum(picks * earlier[:, None, :], axis=2)
    places = (slots[:, :, None] == jnp.arange(CAP, dtype=jnp.int32)[None, None, :]).astype(jnp.float32)
    picked = picks.astype(jnp.float32)
    select = jnp.einsum("ikr,iks->rsi", picked, places, precision=lax.Precision.HIGHEST)
    weigh = jnp.einsum("ikr,iks,ik->rsi", picked, places, gates.astype(jnp.float32), precision=lax.Precision.HIGHEST)
    return select, weigh


def expert_block(operands):
    rows, weight_gate, weight_up, weight_down = operands
    gate = jnp.dot(rows, weight_gate.T, preferred_element_type=jnp.float32)
    upper = jnp.dot(rows, weight_up.T, preferred_element_type=jnp.float32)
    hidden = (jax.nn.silu(gate) * upper).astype(jnp.bfloat16)
    return jnp.dot(hidden, weight_down, preferred_element_type=jnp.float32).astype(jnp.bfloat16)


def reference(tokens, routes, gates, w_gate, w_up, w_down, shared_gate, shared_up, shared_down, vocab, targets):
    grouped = tokens.reshape(N_EXPERT, TOK_E, D)
    select, weigh = jax.vmap(slot_tables)(routes.reshape(N_EXPERT, TOK_E, TOPK), gates.reshape(N_EXPERT, TOK_E, TOPK))
    outgoing = jnp.einsum("grsi,gid->rgsd", select, grouped.astype(jnp.float32), precision=lax.Precision.HIGHEST).astype(jnp.bfloat16)
    rows = outgoing.reshape(EXPERTS, N_EXPERT * CAP, D)
    outputs = lax.map(expert_block, (rows, w_gate, w_up, w_down))
    back = outputs.reshape(EXPERTS, N_EXPERT, CAP, D).astype(jnp.float32)
    routed = jnp.einsum("grsi,rgsd->gid", weigh, back, precision=lax.Precision.HIGHEST).reshape(TOKENS, D)
    shared_g = jnp.dot(tokens, shared_gate.T, preferred_element_type=jnp.float32)
    shared_u = jnp.dot(tokens, shared_up.T, preferred_element_type=jnp.float32)
    shared_hidden = (jax.nn.silu(shared_g) * shared_u).astype(jnp.bfloat16)
    shared_out = jnp.dot(shared_hidden, shared_down, preferred_element_type=jnp.float32)
    layer_out = (tokens.astype(jnp.float32) + shared_out + routed).astype(jnp.bfloat16)
    scored = layer_out.reshape(N_EXPERT, TOK_E, D)[:, TOK_E - SCORE_E:, :].reshape(SCORED, D)
    logits = jnp.dot(scored, vocab.T, preferred_element_type=jnp.float32)
    totals = jnp.sum(jnp.exp(logits), axis=1)
    target_logit = jnp.take_along_axis(logits, targets[:, None].astype(jnp.int32), axis=1)[:, 0]
    return layer_out, target_logit - jnp.log(totals)
```

```python
import jax
import jax.numpy as jnp
from jax import lax
from jax.experimental import pallas as pl
from jax.experimental.pallas import tpu as pltpu
from jax.sharding import PartitionSpec as P

EXPERTS = 16
SCORE_E = 4


def slot_tables(routes, gates, capacity):
    picks = (routes[:, :, None] == jnp.arange(EXPERTS, dtype=jnp.int32)[None, None, :]).astype(
        jnp.int32
    )
    per_token = jnp.sum(picks, axis=1)
    earlier = jnp.cumsum(per_token, axis=0) - per_token
    slots = jnp.sum(picks * earlier[:, None, :], axis=2)
    places = (slots[:, :, None] == jnp.arange(capacity, dtype=jnp.int32)[None, None, :]).astype(
        jnp.float32
    )
    picked = picks.astype(jnp.float32)
    select = jnp.einsum("ikr,iks->rsi", picked, places, precision=lax.Precision.HIGHEST)
    weigh = jnp.einsum("ikr,iks,ik->rsi", picked, places, gates, precision=lax.Precision.HIGHEST)
    return (select.astype(jnp.bfloat16), weigh)


def contract_last(left, right):
    return lax.dot_general(
        left, right, (((1,), (1,)), ((), ())), preferred_element_type=jnp.float32
    )


def shards(
    tokens, routes, gates, w_gate, w_up, w_down, shared_gate, shared_up, shared_down, vocab, targets
):
    tok_rows = tokens.shape[0]
    capacity = tok_rows // 2
    groups = lax.axis_size("expert")
    lanes = lax.axis_size("tensor")
    exp_dev = w_gate.shape[0]
    width = w_gate.shape[1]
    out_width = w_down.shape[2]
    select, weigh = slot_tables(routes, gates, capacity)
    outgoing = jnp.einsum("rsi,id->rsd", select, tokens, preferred_element_type=jnp.float32).astype(
        jnp.bfloat16
    )
    arrived = lax.all_to_all(outgoing, "expert", split_axis=0, concat_axis=1, tiled=True)
    slot_count = arrived.shape[1]
    flat_rows = arrived.reshape(exp_dev * slot_count, arrived.shape[2])
    pieces = (
        lax.all_gather(flat_rows, "tensor", axis=1, tiled=True),
        lax.all_gather(tokens, "tensor", axis=1, tiled=True),
    )
    span = pieces[0].shape[1]
    rows = pieces[0].reshape(exp_dev, slot_count, span)
    gate_acc = jnp.einsum("erw,efw->erf", rows, w_gate, preferred_element_type=jnp.float32)
    up_acc = jnp.einsum("erw,efw->erf", rows, w_up, preferred_element_type=jnp.float32)
    shared_gate_acc = contract_last(pieces[1], shared_gate)
    shared_up_acc = contract_last(pieces[1], shared_up)
    hidden_routed = (jax.nn.silu(gate_acc) * up_acc).astype(jnp.bfloat16)
    hidden_shared = (jax.nn.silu(shared_gate_acc) * shared_up_acc).astype(jnp.bfloat16)
    flat_hidden = hidden_routed.reshape(exp_dev * slot_count, width)
    pieces = (
        lax.all_gather(flat_hidden, "tensor", axis=1, tiled=True),
        lax.all_gather(hidden_shared, "tensor", axis=1, tiled=True),
    )
    span = pieces[0].shape[1]
    rows = pieces[0].reshape(exp_dev, slot_count, span)
    routed_out = jnp.einsum("erw,ewd->erd", rows, w_down, preferred_element_type=jnp.float32)
    shared_out = jnp.dot(pieces[1], shared_down, preferred_element_type=jnp.float32)
    returned = lax.all_to_all(
        routed_out.astype(jnp.bfloat16), "expert", split_axis=1, concat_axis=0, tiled=True
    )
    routed = jnp.einsum(
        "rsi,rsd->id", weigh, returned.astype(jnp.float32), precision=lax.Precision.HIGHEST
    )
    layer_out = (tokens.astype(jnp.float32) + shared_out + routed).astype(jnp.bfloat16)
    scored = layer_out[tok_rows - SCORE_E :].reshape(1, SCORE_E * out_width)
    collected = lax.all_gather(scored, ("expert", "tensor"), axis=0, tiled=True)
    full_rows = (
        collected.reshape(groups, lanes, SCORE_E, out_width)
        .transpose(0, 2, 1, 3)
        .reshape(groups * SCORE_E, lanes * out_width)
    )
    logits = contract_last(full_rows, vocab)
    exp_sums = jnp.sum(jnp.exp(logits), axis=1)
    offset = (lax.axis_index("expert") * lanes + lax.axis_index("tensor")) * vocab.shape[0]
    columns = offset + jnp.arange(vocab.shape[0], dtype=jnp.int32)
    target_part = jnp.sum(jnp.where(targets[:, None] == columns[None, :], logits, 0.0), axis=1)
    totals, target_logit = lax.psum((exp_sums, target_part), ("expert", "tensor"))
    loglik = target_logit - jnp.log(totals)
    return (layer_out, loglik)


MESH_ID = pl.DeviceIdType.MESH
CHUNK_COPIES = 9
NT = (((1,), (1,)), ((), ()))


def flip(index, low):
    return index + low - 2 * low * lax.rem(lax.div(index, low), 2)


def z_peer(z, j):
    for low in (1, 2):
        if j & low:
            z = flip(z, low)
    return z


def t_peer(t, j):
    for low in (1, 2, 4):
        if j & low:
            t = flip(t, low)
    return t


def silu_mul(gate, up):
    return gate / (1.0 + jnp.exp(-gate)) * up


def layer_kernel(
    tokens, routes_t, gates_t, w_gate, w_up, w_down, shared_gate, shared_up, shared_down, vocab, targets,
    out, loglik,
    wg, wu, wd, sg, su, sd, vo, tok, acc_g, acc_u, sh_g, sh_u, hid, out_acc, sh_out, tab, part_out, part_in,
    sc, full, st_t, st_z,
    load_sem, ch_send, ch_recv, z_send, z_recv, t_send, t_recv,
):
    z, t = lax.axis_index("expert"), lax.axis_index("tensor")
    rows, cols = tokens.shape
    cap = rows // 2
    ff = sg.shape[0]

    loads = []
    pairs = (
        (tokens, tok.at[t, pl.ds(z * rows, rows)]), (shared_gate, sg), (shared_up, su), (w_gate, wg), (w_up, wu),
        (w_down, wd), (shared_down, sd), (vocab, vo),
    )
    for i, (a, b) in enumerate(pairs):
        loads.append(pltpu.make_async_copy(a, b, load_sem.at[i]))
        loads[-1].start()

    barrier = pltpu.get_barrier_semaphore()
    for j in range(1, 4):
        pl.semaphore_signal(barrier, inc=1, device_id=(z_peer(z, j), t), device_id_type=MESH_ID)
    for j in range(1, 8):
        pl.semaphore_signal(barrier, inc=1, device_id=(z, t_peer(t, j)), device_id_type=MESH_ID)

    experts = tab.shape[2]
    expert_row = lax.broadcasted_iota(jnp.int32, (experts, rows), 0)
    member = jnp.zeros((experts, rows), jnp.float32)
    weight = jnp.zeros((experts, rows), jnp.float32)
    for k in range(routes_t.shape[0]):
        hit = routes_t[k : k + 1, :] == expert_row
        member = jnp.where(hit, 1.0, member)
        weight = jnp.where(hit, gates_t[k : k + 1, :], weight)
    before = lax.broadcasted_iota(jnp.int32, (rows, rows), 0) < lax.broadcasted_iota(jnp.int32, (rows, rows), 1)
    earlier = jnp.dot(
        member.astype(jnp.bfloat16),
        jnp.where(before, 1.0, 0.0).astype(jnp.bfloat16),
        preferred_element_type=jnp.float32,
    )
    tab[0, 0] = jnp.where(member > 0.5, earlier, -1.0)
    tab[0, 1] = weight

    pl.semaphore_wait(barrier, 10)

    sends = []

    def send(src, dst, ssem, rsem, dev):
        copy = pltpu.make_async_remote_copy(
            src_ref=src, dst_ref=dst, send_sem=ssem, recv_sem=rsem, device_id=dev, device_id_type=MESH_ID
        )
        copy.start()
        sends.append(copy)

    def landed(dst, rsem):
        pltpu.make_async_remote_copy(
            src_ref=dst, dst_ref=dst, send_sem=ch_send.at[0], recv_sem=rsem, device_id=(z, t_peer(t, 1)),
            device_id_type=MESH_ID,
        ).wait_recv()

    t_c, t_x, t_y, t_d = t_peer(t, 1), t_peer(t, 2), t_peer(t, 4), t_peer(t, 6)

    class Chunk:
        def __init__(self, number, buf, start, count):
            self.base, self.buf, self.first, self.count = number * CHUNK_COPIES, buf, start, count

        def part(self, owner, which=None):
            if which is None:
                return self.buf.at[owner, pl.ds(self.first, self.count)]
            half = self.count // 2
            return self.buf.at[owner, pl.ds(self.first + which * half, half)]

        def go(self, ref, n, peer):
            send(ref, ref, ch_send.at[self.base + n], ch_recv.at[self.base + n], (z, peer))

        def got(self, ref, n):
            landed(ref, ch_recv.at[self.base + n])

        def start(self):
            for n, peer in ((0, t_x), (1, t_y), (2, t_c)):
                self.go(self.part(t), n, peer)

        def relay(self):
            self.got(self.part(t_x), 0)
            self.go(self.part(t_x, 0), 3, t_y)
            self.go(self.part(t_x), 4, t_c)
            self.got(self.part(t_y), 1)
            self.go(self.part(t_y, 1), 5, t_x)
            self.go(self.part(t_y), 6, t_c)

        def relay_far(self):
            self.got(self.part(t_d, 0), 3)
            self.go(self.part(t_d, 0), 7, t_c)
            self.got(self.part(t_d, 1), 5)
            self.go(self.part(t_d, 1), 8, t_c)

        def wait_own(self):
            self.got(self.part(t_c), 2)

        def wait_x(self):
            self.got(self.part(t_peer(t, 3)), 4)

        def wait_y(self):
            self.got(self.part(t_peer(t, 5)), 6)

        def wait_far(self):
            self.got(self.part(t_peer(t, 7), 0), 7)
            self.got(self.part(t_peer(t, 7), 1), 8)

        def finish(self):
            self.wait_own()
            self.wait_x()
            self.wait_y()
            self.wait_far()

    groups = [z, z_peer(z, 1), z_peer(z, 2), z_peer(z, 3)]
    chunks = [Chunk(k, tok, groups[k] * rows, rows) for k in range(4)]
    far_rows, own_rows = 8 * cap // 2, 8 * cap // 2 + cap
    hid_far = Chunk(4, hid, 0, far_rows)
    hid_own = Chunk(5, hid, far_rows, own_rows)
    loads[0].wait()
    for j in (1, 2, 3):
        mine = tok.at[t, pl.ds(z * rows, rows)]
        send(mine, mine, z_send.at[j], z_recv.at[j], (groups[j], t))
    for j in (1, 2, 3):
        send(tab.at[0], tab.at[j], z_send.at[4 + j], z_recv.at[4 + j], (groups[j], t))
    chunks[0].start()

    def z_landed(j):
        landed(chunks[j].part(t), z_recv.at[j])
        chunks[j].start()

    z_landed(1)
    chunks[0].relay()
    z_landed(2)
    chunks[1].relay()
    chunks[0].relay_far()
    z_landed(3)
    for load in loads[1:5]:
        load.wait()
    chunks[1].relay_far()
    chunks[0].finish()
    chunks[1].finish()

    def clear():
        acc_g[...] = jnp.zeros_like(acc_g)
        acc_u[...] = jnp.zeros_like(acc_u)

    def up_seg(pair, chip, shared):
        def step(i, carry):
            owner = 2 * chip + i
            span = pl.ds(pl.multiple_of(owner * cols, 128), cols)
            x = tok[owner, pl.ds(pl.multiple_of(pair * 2 * rows, 128), 2 * rows), :]
            acc_g[...] += lax.dot_general(x, wg[:, span], NT, preferred_element_type=jnp.float32)
            acc_u[...] += lax.dot_general(x, wu[:, span], NT, preferred_element_type=jnp.float32)
            if shared:
                own = tok[owner, pl.ds(pl.multiple_of(z * rows, 128), rows), :]
                sh_g[...] += lax.dot_general(own, sg[:, span], NT, preferred_element_type=jnp.float32)
                sh_u[...] += lax.dot_general(own, su[:, span], NT, preferred_element_type=jnp.float32)
            return carry

        lax.fori_loop(0, 2, step, 0)

    slot_no = lax.broadcasted_iota(jnp.int32, (cap, rows), 0).astype(jnp.float32)

    def table_of(j):
        first = pl.ds(4 * z, 4)
        return tab[j, 0, first, :], tab[j, 1, first, :]

    def squeeze(first_row, js):
        for j in js:
            place = lax.rem(groups[j], 2)
            span = pl.ds(pl.multiple_of(place * rows, 128), rows)
            h = silu_mul(acc_g[span, :], acc_u[span, :]).astype(jnp.bfloat16)
            slots, _ = table_of(j)
            for q in range(2):
                both = h[:, 2 * q * ff : 2 * (q + 1) * ff]
                picked = []
                for e in (2 * q, 2 * q + 1):
                    sel = jnp.where(slot_no == slots[e : e + 1, :], 1.0, 0.0).astype(jnp.bfloat16)
                    picked.append(jnp.dot(sel, both, preferred_element_type=jnp.float32))
                lane = lax.broadcasted_iota(jnp.int32, picked[0].shape, 1)
                at = pl.ds(pl.multiple_of(first_row + q * 2 * cap + place * cap, 16), cap)
                hid[t, at, :] = jnp.where(lane < ff, picked[0], picked[1]).astype(jnp.bfloat16)

    chip, chip_x, chip_y, chip_d = [lax.div(v, 2) for v in (t, t_x, t_y, t_d)]
    own_pair, far_pair = lax.div(z, 2), 1 - lax.div(z, 2)
    clear()
    sh_g[...] = jnp.zeros_like(sh_g)
    sh_u[...] = jnp.zeros_like(sh_u)
    up_seg(own_pair, chip, True)
    chunks[2].relay()
    up_seg(own_pair, chip_x, True)
    up_seg(own_pair, chip_y, True)
    chunks[3].relay()
    chunks[2].relay_far()
    up_seg(own_pair, chip_d, True)
    for j in (1, 2, 3):
        landed(tab.at[j], z_recv.at[4 + j])
    squeeze(far_rows, (0, 1))
    hs = silu_mul(sh_g[...], sh_u[...])
    hid[t, pl.ds(2 * far_rows, cap), :] = jnp.concatenate([hs[:cap], hs[cap:]], axis=1).astype(jnp.bfloat16)
    clear()
    chunks[3].relay_far()
    for c in (2, 3):
        chunks[c].wait_own()
    up_seg(far_pair, chip, False)
    for c in (2, 3):
        chunks[c].wait_x()
    up_seg(far_pair, chip_x, False)
    for c in (2, 3):
        chunks[c].wait_y()
    up_seg(far_pair, chip_y, False)
    for c in (2, 3):
        chunks[c].wait_far()
    up_seg(far_pair, chip_d, False)
    squeeze(0, (2, 3))
    hid_far.start()
    hid_own.start()
    for load in loads[5:]:
        load.wait()

    def down_seg(first_row, chip_no, shared):
        def step(i, carry):
            owner = 2 * chip_no + i
            span = pl.ds(pl.multiple_of(owner * ff, 16), ff)
            for q in range(2):
                h = hid[owner, pl.ds(first_row + q * 2 * cap, 2 * cap), :]
                for k in range(2):
                    out_acc[2 * q + k] += jnp.dot(
                        h[:, k * ff : (k + 1) * ff], wd[2 * q + k, span, :], preferred_element_type=jnp.float32
                    )
            if shared:
                h = hid[owner, pl.ds(2 * far_rows, cap), :]
                for k in range(2):
                    sh_out[k * cap : (k + 1) * cap, :] += jnp.dot(
                        h[:, k * ff : (k + 1) * ff], sd[span, :], preferred_element_type=jnp.float32
                    )
            return carry

        lax.fori_loop(0, 2, step, 0)

    def combine(j):
        place = lax.rem(groups[j], 2)
        span = pl.ds(pl.multiple_of(place * cap, 16), cap)
        slots, weights = table_of(j)
        ys = jnp.concatenate([out_acc[e, span, :].astype(jnp.bfloat16) for e in range(4)], axis=0)
        mix = jnp.concatenate(
            [jnp.where(slot_no == slots[e : e + 1, :], weights[e : e + 1, :], 0.0) for e in range(4)], axis=0
        ).T
        high = mix.astype(jnp.bfloat16)
        low = (mix - high.astype(jnp.float32)).astype(jnp.bfloat16)
        return jnp.dot(high, ys, preferred_element_type=jnp.float32) + jnp.dot(
            low, ys, preferred_element_type=jnp.float32
        )

    def give(j):
        part_out[j] = combine(j).astype(jnp.bfloat16)
        send(part_out.at[j], part_in.at[j], z_send.at[8 + j], z_recv.at[8 + j], (groups[j], t))

    out_acc[...] = jnp.zeros_like(out_acc)
    sh_out[...] = jnp.zeros_like(sh_out)
    hid_far.wait_own()
    down_seg(0, chip, False)
    hid_far.relay()
    hid_far.wait_x()
    down_seg(0, chip_x, False)
    hid_far.relay_far()
    hid_far.wait_y()
    down_seg(0, chip_y, False)
    hid_far.wait_far()
    down_seg(0, chip_d, False)
    hid_own.relay()
    give(2)
    give(3)
    out_acc[...] = jnp.zeros_like(out_acc)
    hid_own.wait_own()
    down_seg(far_rows, chip, True)
    hid_own.relay_far()
    hid_own.wait_x()
    down_seg(far_rows, chip_x, True)
    hid_own.wait_y()
    down_seg(far_rows, chip_y, True)
    hid_own.wait_far()
    down_seg(far_rows, chip_d, True)
    give(1)
    total = tok[t, pl.ds(pl.multiple_of(z * rows, 128), rows), :].astype(jnp.float32) + sh_out[...] + combine(0)
    for j in (1, 2, 3):
        landed(part_in.at[j], z_recv.at[8 + j])
        total += part_in[j].astype(jnp.float32)
    layer = total.astype(jnp.bfloat16)
    out[...] = layer

    sc[z] = layer[rows - 16 :, :]
    for j in (1, 2, 3):
        send(sc.at[z], sc.at[z], z_send.at[12 + j], z_recv.at[12 + j], (groups[j], t))
    for j in (1, 2, 3):
        landed(sc.at[groups[j]], z_recv.at[12 + j])
    full[t] = jnp.concatenate(
        [sc[g].astype(jnp.float32)[16 - SCORE_E :, :] for g in range(4)], axis=0
    ).astype(jnp.bfloat16)
    for j in range(1, 8):
        send(full.at[t], full.at[t], t_send.at[j], t_recv.at[j], (z, t_peer(t, j)))
    logits = jnp.zeros((vo.shape[0], full.shape[1]), jnp.float32)
    for j in range(8):
        owner = t_peer(t, j)
        if j:
            landed(full.at[owner], t_recv.at[j])
        span = pl.ds(pl.multiple_of(owner * cols, 128), cols)
        logits += lax.dot_general(vo[:, span], full[owner], NT, preferred_element_type=jnp.float32)
    offset = (z * 8 + t) * vo.shape[0]
    entry = offset + lax.broadcasted_iota(jnp.int32, logits.shape, 0)
    st_t[0] = jnp.zeros_like(st_t[0])
    st_t[0, 0:1, 0:16] = jnp.sum(jnp.exp(logits), axis=0, keepdims=True)
    st_t[0, 1:2, 0:16] = jnp.sum(jnp.where(entry == targets[...], logits, 0.0), axis=0, keepdims=True)
    for j in range(1, 8):
        send(st_t.at[0], st_t.at[j], t_send.at[8 + j], t_recv.at[8 + j], (z, t_peer(t, j)))
    summed = st_t[0]
    for j in range(1, 8):
        landed(st_t.at[j], t_recv.at[8 + j])
        summed += st_t[j]
    st_z[z] = summed
    for j in (1, 2, 3):
        send(st_z.at[z], st_z.at[z], z_send.at[16 + j], z_recv.at[16 + j], (groups[j], t))
    for j in (1, 2, 3):
        landed(st_z.at[groups[j]], z_recv.at[16 + j])
    both = ((st_z[0] + st_z[1]) + st_z[2]) + st_z[3]
    loglik[...] = both[1:2, 0:16] - jnp.log(both[0:1, 0:16])
    for copy in sends:
        copy.wait_send()


def fused_shards(
    tokens, routes, gates, w_gate, w_up, w_down, shared_gate, shared_up, shared_down, vocab, targets
):
    rows, cols = tokens.shape
    own, ff, depth = w_gate.shape
    cap = rows // 2
    far_rows = 4 * cap
    bf, f32 = jnp.bfloat16, jnp.float32
    hbm, vmem = pl.BlockSpec(memory_space=pl.ANY), pl.BlockSpec(memory_space=pltpu.VMEM)
    dma = pltpu.SemaphoreType.DMA
    out, loglik = pl.pallas_call(
        layer_kernel,
        out_shape=(jax.ShapeDtypeStruct((rows, cols), bf), jax.ShapeDtypeStruct((1, targets.shape[0]), f32)),
        in_specs=[hbm, vmem, vmem, hbm, hbm, hbm, hbm, hbm, hbm, hbm, vmem],
        out_specs=(vmem, vmem),
        scratch_shapes=[
            pltpu.VMEM((own * ff, depth), bf),
            pltpu.VMEM((own * ff, depth), bf),
            pltpu.VMEM(w_down.shape, bf),
            pltpu.VMEM(shared_gate.shape, bf),
            pltpu.VMEM(shared_up.shape, bf),
            pltpu.VMEM(shared_down.shape, bf),
            pltpu.VMEM(vocab.shape, bf),
            pltpu.VMEM((8, 4 * rows, cols), bf),
            pltpu.VMEM((2 * rows, own * ff), f32),
            pltpu.VMEM((2 * rows, own * ff), f32),
            pltpu.VMEM((rows, ff), f32),
            pltpu.VMEM((rows, ff), f32),
            pltpu.VMEM((8, 2 * far_rows + cap, 2 * ff), bf),
            pltpu.VMEM((own, 2 * cap, cols), f32),
            pltpu.VMEM((rows, cols), f32),
            pltpu.VMEM((4, 2, EXPERTS, rows), f32),
            pltpu.VMEM((4, rows, cols), bf),
            pltpu.VMEM((4, rows, cols), bf),
            pltpu.VMEM((4, 16, cols), bf),
            pltpu.VMEM((8, 4 * SCORE_E, cols), bf),
            pltpu.VMEM((8, 8, 128), f32),
            pltpu.VMEM((4, 8, 128), f32),
            dma((8,)),
            dma((6 * CHUNK_COPIES,)),
            dma((6 * CHUNK_COPIES,)),
            dma((20,)),
            dma((20,)),
            dma((16,)),
            dma((16,)),
        ],
        compiler_params=pltpu.CompilerParams(
            collective_id=0, has_side_effects=True, vmem_limit_bytes=60 * 2**20
        ),
    )(
        tokens, routes.T, gates.T, w_gate.reshape(own * ff, depth), w_up.reshape(own * ff, depth), w_down,
        shared_gate, shared_up, shared_down, vocab, targets.reshape(1, -1),
    )
    return out, loglik.reshape(-1)


def solution(mesh):
    placed = (
        P("expert", "tensor"),
        P("expert", None),
        P("expert", None),
        P("expert", "tensor", None),
        P("expert", "tensor", None),
        P("expert", None, "tensor"),
        P("tensor", None),
        P("tensor", None),
        P(None, "tensor"),
        P(("expert", "tensor"), None),
        P(),
    )
    fits = mesh.shape["expert"] == 4 and mesh.shape["tensor"] == 8
    return jax.shard_map(
        fused_shards if fits else shards, mesh=mesh, in_specs=placed, out_specs=(P("expert", "tensor"), P()), check_vma=False
    )
```

```python
import jax
import jax.numpy as jnp
from jax import lax
from jax.experimental import pallas as pl
from jax.experimental.pallas import tpu as pltpu
from jax.sharding import PartitionSpec as P

EXPERTS = 16
SCORE_E = 4


def slot_tables(routes, gates, capacity):
    picks = (routes[:, :, None] == jnp.arange(EXPERTS, dtype=jnp.int32)[None, None, :]).astype(
        jnp.int32
    )
    per_token = jnp.sum(picks, axis=1)
    earlier = jnp.cumsum(per_token, axis=0) - per_token
    slots = jnp.sum(picks * earlier[:, None, :], axis=2)
    places = (slots[:, :, None] == jnp.arange(capacity, dtype=jnp.int32)[None, None, :]).astype(
        jnp.float32
    )
    picked = picks.astype(jnp.float32)
    select = jnp.einsum("ikr,iks->rsi", picked, places, precision=lax.Precision.HIGHEST)
    weigh = jnp.einsum("ikr,iks,ik->rsi", picked, places, gates, precision=lax.Precision.HIGHEST)
    return (select.astype(jnp.bfloat16), weigh)


def contract_last(left, right):
    return lax.dot_general(
        left, right, (((1,), (1,)), ((), ())), preferred_element_type=jnp.float32
    )


def shards(
    tokens, routes, gates, w_gate, w_up, w_down, shared_gate, shared_up, shared_down, vocab, targets
):
    tok_rows = tokens.shape[0]
    capacity = tok_rows // 2
    groups = lax.axis_size("expert")
    lanes = lax.axis_size("tensor")
    exp_dev = w_gate.shape[0]
    width = w_gate.shape[1]
    out_width = w_down.shape[2]
    select, weigh = slot_tables(routes, gates, capacity)
    outgoing = jnp.einsum("rsi,id->rsd", select, tokens, preferred_element_type=jnp.float32).astype(
        jnp.bfloat16
    )
    arrived = lax.all_to_all(outgoing, "expert", split_axis=0, concat_axis=1, tiled=True)
    slot_count = arrived.shape[1]
    flat_rows = arrived.reshape(exp_dev * slot_count, arrived.shape[2])
    pieces = (
        lax.all_gather(flat_rows, "tensor", axis=1, tiled=True),
        lax.all_gather(tokens, "tensor", axis=1, tiled=True),
    )
    span = pieces[0].shape[1]
    rows = pieces[0].reshape(exp_dev, slot_count, span)
    gate_acc = jnp.einsum("erw,efw->erf", rows, w_gate, preferred_element_type=jnp.float32)
    up_acc = jnp.einsum("erw,efw->erf", rows, w_up, preferred_element_type=jnp.float32)
    shared_gate_acc = contract_last(pieces[1], shared_gate)
    shared_up_acc = contract_last(pieces[1], shared_up)
    hidden_routed = (jax.nn.silu(gate_acc) * up_acc).astype(jnp.bfloat16)
    hidden_shared = (jax.nn.silu(shared_gate_acc) * shared_up_acc).astype(jnp.bfloat16)
    flat_hidden = hidden_routed.reshape(exp_dev * slot_count, width)
    pieces = (
        lax.all_gather(flat_hidden, "tensor", axis=1, tiled=True),
        lax.all_gather(hidden_shared, "tensor", axis=1, tiled=True),
    )
    span = pieces[0].shape[1]
    rows = pieces[0].reshape(exp_dev, slot_count, span)
    routed_out = jnp.einsum("erw,ewd->erd", rows, w_down, preferred_element_type=jnp.float32)
    shared_out = jnp.dot(pieces[1], shared_down, preferred_element_type=jnp.float32)
    returned = lax.all_to_all(
        routed_out.astype(jnp.bfloat16), "expert", split_axis=1, concat_axis=0, tiled=True
    )
    routed = jnp.einsum(
        "rsi,rsd->id", weigh, returned.astype(jnp.float32), precision=lax.Precision.HIGHEST
    )
    layer_out = (tokens.astype(jnp.float32) + shared_out + routed).astype(jnp.bfloat16)
    scored = layer_out[tok_rows - SCORE_E :].reshape(1, SCORE_E * out_width)
    collected = lax.all_gather(scored, ("expert", "tensor"), axis=0, tiled=True)
    full_rows = (
        collected.reshape(groups, lanes, SCORE_E, out_width)
        .transpose(0, 2, 1, 3)
        .reshape(groups * SCORE_E, lanes * out_width)
    )
    logits = contract_last(full_rows, vocab)
    exp_sums = jnp.sum(jnp.exp(logits), axis=1)
    offset = (lax.axis_index("expert") * lanes + lax.axis_index("tensor")) * vocab.shape[0]
    columns = offset + jnp.arange(vocab.shape[0], dtype=jnp.int32)
    target_part = jnp.sum(jnp.where(targets[:, None] == columns[None, :], logits, 0.0), axis=1)
    totals, target_logit = lax.psum((exp_sums, target_part), ("expert", "tensor"))
    loglik = target_logit - jnp.log(totals)
    return (layer_out, loglik)


MESH_ID = pl.DeviceIdType.MESH
CHUNK_COPIES = 9
NT = (((1,), (1,)), ((), ()))


def flip(index, low):
    return index + low - 2 * low * lax.rem(lax.div(index, low), 2)


def z_peer(z, j):
    for low in (1, 2):
        if j & low:
            z = flip(z, low)
    return z


def t_peer(t, j):
    for low in (1, 2, 4):
        if j & low:
            t = flip(t, low)
    return t


def silu_mul(gate, up):
    return gate / (1.0 + jnp.exp(-gate)) * up


def layer_kernel(
    tokens, routes_t, gates_t, w_gate, w_up, w_down, shared_gate, shared_up, shared_down, vocab, targets,
    out, loglik,
    wg, wu, wd, sg, su, sd, vo, tok, acc_g, acc_u, sh_g, sh_u, hid, out_acc, sh_out, tab, part_out, part_in,
    sc, full, st_t, st_z,
    load_sem, ch_send, ch_recv, z_send, z_recv, t_send, t_recv,
):
    z, t = lax.axis_index("expert"), lax.axis_index("tensor")
    rows, cols = tokens.shape
    cap = rows // 2
    ff = sg.shape[0]

    loads = []
    pairs = (
        (tokens, tok.at[t, pl.ds(z * rows, rows)]), (shared_gate, sg), (shared_up, su), (w_gate, wg), (w_up, wu),
        (w_down, wd), (shared_down, sd), (vocab, vo),
    )
    for i, (a, b) in enumerate(pairs):
        loads.append(pltpu.make_async_copy(a, b, load_sem.at[i]))
        loads[-1].start()

    barrier = pltpu.get_barrier_semaphore()
    for j in range(1, 4):
        pl.semaphore_signal(barrier, inc=1, device_id=(z_peer(z, j), t), device_id_type=MESH_ID)
    for j in range(1, 8):
        pl.semaphore_signal(barrier, inc=1, device_id=(z, t_peer(t, j)), device_id_type=MESH_ID)

    experts = tab.shape[2]
    expert_row = lax.broadcasted_iota(jnp.int32, (experts, rows), 0)
    member = jnp.zeros((experts, rows), jnp.float32)
    weight = jnp.zeros((experts, rows), jnp.float32)
    for k in range(routes_t.shape[0]):
        hit = routes_t[k : k + 1, :] == expert_row
        member = jnp.where(hit, 1.0, member)
        weight = jnp.where(hit, gates_t[k : k + 1, :], weight)
    before = lax.broadcasted_iota(jnp.int32, (rows, rows), 0) < lax.broadcasted_iota(jnp.int32, (rows, rows), 1)
    earlier = jnp.dot(
        member.astype(jnp.bfloat16),
        jnp.where(before, 1.0, 0.0).astype(jnp.bfloat16),
        preferred_element_type=jnp.float32,
    )
    tab[0, 0] = jnp.where(member > 0.5, earlier, -1.0)
    tab[0, 1] = weight

    pl.semaphore_wait(barrier, 10)

    sends = []

    def send(src, dst, ssem, rsem, dev):
        copy = pltpu.make_async_remote_copy(
            src_ref=src, dst_ref=dst, send_sem=ssem, recv_sem=rsem, device_id=dev, device_id_type=MESH_ID
        )
        copy.start()
        sends.append(copy)

    def landed(dst, rsem):
        pltpu.make_async_remote_copy(
            src_ref=dst, dst_ref=dst, send_sem=ch_send.at[0], recv_sem=rsem, device_id=(z, t_peer(t, 1)),
            device_id_type=MESH_ID,
        ).wait_recv()

    t_c, t_x, t_y, t_d = t_peer(t, 1), t_peer(t, 2), t_peer(t, 4), t_peer(t, 6)

    class Chunk:
        def __init__(self, number, buf, start, count):
            self.base, self.buf, self.first, self.count = number * CHUNK_COPIES, buf, start, count

        def part(self, owner, which=None):
            if which is None:
                return self.buf.at[owner, pl.ds(self.first, self.count)]
            half = self.count // 2
            return self.buf.at[owner, pl.ds(self.first + which * half, half)]

        def go(self, ref, n, peer):
            send(ref, ref, ch_send.at[self.base + n], ch_recv.at[self.base + n], (z, peer))

        def got(self, ref, n):
            landed(ref, ch_recv.at[self.base + n])

        def start(self):
            for n, peer in ((0, t_x), (1, t_y), (2, t_c)):
                self.go(self.part(t), n, peer)

        def relay(self):
            self.got(self.part(t_x), 0)
            self.go(self.part(t_x, 0), 3, t_y)
            self.go(self.part(t_x), 4, t_c)
            self.got(self.part(t_y), 1)
            self.go(self.part(t_y, 1), 5, t_x)
            self.go(self.part(t_y), 6, t_c)

        def relay_far(self):
            self.got(self.part(t_d, 0), 3)
            self.go(self.part(t_d, 0), 7, t_c)
            self.got(self.part(t_d, 1), 5)
            self.go(self.part(t_d, 1), 8, t_c)

        def wait_own(self):
            self.got(self.part(t_c), 2)

        def wait_x(self):
            self.got(self.part(t_peer(t, 3)), 4)

        def wait_y(self):
            self.got(self.part(t_peer(t, 5)), 6)

        def wait_far(self):
            self.got(self.part(t_peer(t, 7), 0), 7)
            self.got(self.part(t_peer(t, 7), 1), 8)

        def finish(self):
            self.wait_own()
            self.wait_x()
            self.wait_y()
            self.wait_far()

    groups = [z, z_peer(z, 1), z_peer(z, 2), z_peer(z, 3)]
    chunks = [Chunk(k, tok, groups[k] * rows, rows) for k in range(4)]
    far_rows, own_rows = 8 * cap // 2, 8 * cap // 2 + cap
    hid_far = Chunk(4, hid, 0, far_rows)
    hid_own = Chunk(5, hid, far_rows, own_rows)
    loads[0].wait()
    for j in (1, 2, 3):
        mine = tok.at[t, pl.ds(z * rows, rows)]
        send(mine, mine, z_send.at[j], z_recv.at[j], (groups[j], t))
    for j in (1, 2, 3):
        send(tab.at[0], tab.at[j], z_send.at[4 + j], z_recv.at[4 + j], (groups[j], t))
    chunks[0].start()

    def z_landed(j):
        landed(chunks[j].part(t), z_recv.at[j])
        chunks[j].start()

    z_landed(1)
    chunks[0].relay()
    chunks[1].relay()
    chunks[0].relay_far()
    chunks[1].relay_far()
    for load in loads[1:5]:
        load.wait()
    chunks[0].finish()
    chunks[1].finish()

    def clear():
        acc_g[...] = jnp.zeros_like(acc_g)
        acc_u[...] = jnp.zeros_like(acc_u)

    def up_seg(pair, chip, shared):
        def step(i, carry):
            owner = 2 * chip + i
            span = pl.ds(pl.multiple_of(owner * cols, 128), cols)
            x = tok[owner, pl.ds(pl.multiple_of(pair * 2 * rows, 128), 2 * rows), :]
            acc_g[...] += lax.dot_general(x, wg[:, span], NT, preferred_element_type=jnp.float32)
            acc_u[...] += lax.dot_general(x, wu[:, span], NT, preferred_element_type=jnp.float32)
            if shared:
                own = tok[owner, pl.ds(pl.multiple_of(z * rows, 128), rows), :]
                sh_g[...] += lax.dot_general(own, sg[:, span], NT, preferred_element_type=jnp.float32)
                sh_u[...] += lax.dot_general(own, su[:, span], NT, preferred_element_type=jnp.float32)
            return carry

        lax.fori_loop(0, 2, step, 0)

    slot_no = lax.broadcasted_iota(jnp.int32, (cap, rows), 0).astype(jnp.float32)

    def table_of(j):
        first = pl.ds(4 * z, 4)
        return tab[j, 0, first, :], tab[j, 1, first, :]

    def squeeze(first_row, js):
        for j in js:
            place = lax.rem(groups[j], 2)
            span = pl.ds(pl.multiple_of(place * rows, 128), rows)
            h = silu_mul(acc_g[span, :], acc_u[span, :]).astype(jnp.bfloat16)
            slots, _ = table_of(j)
            for q in range(2):
                both = h[:, 2 * q * ff : 2 * (q + 1) * ff]
                picked = []
                for e in (2 * q, 2 * q + 1):
                    sel = jnp.where(slot_no == slots[e : e + 1, :], 1.0, 0.0).astype(jnp.bfloat16)
                    picked.append(jnp.dot(sel, both, preferred_element_type=jnp.float32))
                lane = lax.broadcasted_iota(jnp.int32, picked[0].shape, 1)
                at = pl.ds(pl.multiple_of(first_row + q * 2 * cap + place * cap, 16), cap)
                hid[t, at, :] = jnp.where(lane < ff, picked[0], picked[1]).astype(jnp.bfloat16)

    chip, chip_x, chip_y, chip_d = [lax.div(v, 2) for v in (t, t_x, t_y, t_d)]
    own_pair, far_pair = lax.div(z, 2), 1 - lax.div(z, 2)
    clear()
    sh_g[...] = jnp.zeros_like(sh_g)
    sh_u[...] = jnp.zeros_like(sh_u)
    up_seg(own_pair, chip, True)
    z_landed(2)
    up_seg(own_pair, chip_x, True)
    z_landed(3)
    chunks[2].relay()
    up_seg(own_pair, chip_y, True)
    chunks[3].relay()
    chunks[2].relay_far()
    up_seg(own_pair, chip_d, True)
    for j in (1, 2, 3):
        landed(tab.at[j], z_recv.at[4 + j])
    squeeze(far_rows, (0, 1))
    hs = silu_mul(sh_g[...], sh_u[...])
    hid[t, pl.ds(2 * far_rows, cap), :] = jnp.concatenate([hs[:cap], hs[cap:]], axis=1).astype(jnp.bfloat16)
    clear()
    chunks[3].relay_far()
    for c in (2, 3):
        chunks[c].wait_own()
    up_seg(far_pair, chip, False)
    for c in (2, 3):
        chunks[c].wait_x()
    up_seg(far_pair, chip_x, False)
    for c in (2, 3):
        chunks[c].wait_y()
    up_seg(far_pair, chip_y, False)
    for c in (2, 3):
        chunks[c].wait_far()
    up_seg(far_pair, chip_d, False)
    squeeze(0, (2, 3))
    hid_far.start()
    hid_own.start()
    for load in loads[5:]:
        load.wait()

    def down_seg(first_row, chip_no, shared):
        def step(i, carry):
            owner = 2 * chip_no + i
            span = pl.ds(pl.multiple_of(owner * ff, 16), ff)
            for q in range(2):
                h = hid[owner, pl.ds(first_row + q * 2 * cap, 2 * cap), :]
                for k in range(2):
                    out_acc[2 * q + k] += jnp.dot(
                        h[:, k * ff : (k + 1) * ff], wd[2 * q + k, span, :], preferred_element_type=jnp.float32
                    )
            if shared:
                h = hid[owner, pl.ds(2 * far_rows, cap), :]
                for k in range(2):
                    sh_out[k * cap : (k + 1) * cap, :] += jnp.dot(
                        h[:, k * ff : (k + 1) * ff], sd[span, :], preferred_element_type=jnp.float32
                    )
            return carry

        lax.fori_loop(0, 2, step, 0)

    def combine(j):
        place = lax.rem(groups[j], 2)
        span = pl.ds(pl.multiple_of(place * cap, 16), cap)
        slots, weights = table_of(j)
        ys = jnp.concatenate([out_acc[e, span, :].astype(jnp.bfloat16) for e in range(4)], axis=0)
        mix = jnp.concatenate(
            [jnp.where(slot_no == slots[e : e + 1, :], weights[e : e + 1, :], 0.0) for e in range(4)], axis=0
        ).T
        high = mix.astype(jnp.bfloat16)
        low = (mix - high.astype(jnp.float32)).astype(jnp.bfloat16)
        return jnp.dot(high, ys, preferred_element_type=jnp.float32) + jnp.dot(
            low, ys, preferred_element_type=jnp.float32
        )

    ends, rest = pl.ds(rows - 16, 16), pl.ds(0, rows - 16)

    def give(js):
        for j in js:
            part_out[j] = combine(j).astype(jnp.bfloat16)
        for at, first in ((ends, 8), (rest, 20)):
            for j in js:
                send(
                    part_out.at[j, at], part_in.at[j, at], z_send.at[first + j], z_recv.at[first + j], (groups[j], t)
                )

    out_acc[...] = jnp.zeros_like(out_acc)
    sh_out[...] = jnp.zeros_like(sh_out)
    hid_far.wait_own()
    down_seg(0, chip, False)
    hid_far.relay()
    hid_far.wait_x()
    down_seg(0, chip_x, False)
    hid_far.relay_far()
    hid_far.wait_y()
    down_seg(0, chip_y, False)
    hid_far.wait_far()
    down_seg(0, chip_d, False)
    hid_own.relay()
    give((2, 3))
    out_acc[...] = jnp.zeros_like(out_acc)
    hid_own.wait_own()
    down_seg(far_rows, chip, True)
    hid_own.relay_far()
    hid_own.wait_x()
    down_seg(far_rows, chip_x, True)
    hid_own.wait_y()
    down_seg(far_rows, chip_y, True)
    hid_own.wait_far()
    down_seg(far_rows, chip_d, True)
    give((1,))
    total = tok[t, pl.ds(pl.multiple_of(z * rows, 128), rows), :].astype(jnp.float32) + sh_out[...] + combine(0)
    last = total[rows - 16 :, :]
    sh_out[...] = total
    for j in (1, 2, 3):
        landed(part_in.at[j, ends], z_recv.at[8 + j])
        last += part_in[j, rows - 16 :, :].astype(jnp.float32)
    layer_end = last.astype(jnp.bfloat16)
    out[rows - 16 :, :] = layer_end

    sc[z] = layer_end
    for j in (1, 2, 3):
        send(sc.at[z], sc.at[z], z_send.at[12 + j], z_recv.at[12 + j], (groups[j], t))
    for j in (1, 2, 3):
        landed(sc.at[groups[j]], z_recv.at[12 + j])
    full[t] = jnp.concatenate(
        [sc[g].astype(jnp.float32)[16 - SCORE_E :, :] for g in range(4)], axis=0
    ).astype(jnp.bfloat16)
    for j in range(1, 8):
        send(full.at[t], full.at[t], t_send.at[j], t_recv.at[j], (z, t_peer(t, j)))
    logits = jnp.zeros((vo.shape[0], full.shape[1]), jnp.float32)
    for j in range(8):
        owner = t_peer(t, j)
        if j:
            landed(full.at[owner], t_recv.at[j])
        span = pl.ds(pl.multiple_of(owner * cols, 128), cols)
        logits += lax.dot_general(vo[:, span], full[owner], NT, preferred_element_type=jnp.float32)
    offset = (z * 8 + t) * vo.shape[0]
    entry = offset + lax.broadcasted_iota(jnp.int32, logits.shape, 0)
    st_t[0] = jnp.zeros_like(st_t[0])
    st_t[0, 0:1, 0:16] = jnp.sum(jnp.exp(logits), axis=0, keepdims=True)
    st_t[0, 1:2, 0:16] = jnp.sum(jnp.where(entry == targets[...], logits, 0.0), axis=0, keepdims=True)
    for j in range(1, 8):
        send(st_t.at[0], st_t.at[j], t_send.at[8 + j], t_recv.at[8 + j], (z, t_peer(t, j)))
    summed = st_t[0]
    for j in range(1, 8):
        landed(st_t.at[j], t_recv.at[8 + j])
        summed += st_t[j]
    st_z[z] = summed
    for j in (1, 2, 3):
        send(st_z.at[z], st_z.at[z], z_send.at[16 + j], z_recv.at[16 + j], (groups[j], t))
    body = sh_out[0 : rows - 16, :]
    for j in (1, 2, 3):
        landed(part_in.at[j, rest], z_recv.at[20 + j])
        body += part_in[j, 0 : rows - 16, :].astype(jnp.float32)
    out[0 : rows - 16, :] = body.astype(jnp.bfloat16)
    for j in (1, 2, 3):
        landed(st_z.at[groups[j]], z_recv.at[16 + j])
    both = ((st_z[0] + st_z[1]) + st_z[2]) + st_z[3]
    loglik[...] = both[1:2, 0:16] - jnp.log(both[0:1, 0:16])
    for copy in sends:
        copy.wait_send()


def fused_shards(
    tokens, routes, gates, w_gate, w_up, w_down, shared_gate, shared_up, shared_down, vocab, targets
):
    rows, cols = tokens.shape
    own, ff, depth = w_gate.shape
    cap = rows // 2
    far_rows = 4 * cap
    bf, f32 = jnp.bfloat16, jnp.float32
    hbm, vmem = pl.BlockSpec(memory_space=pl.ANY), pl.BlockSpec(memory_space=pltpu.VMEM)
    dma = pltpu.SemaphoreType.DMA
    out, loglik = pl.pallas_call(
        layer_kernel,
        out_shape=(jax.ShapeDtypeStruct((rows, cols), bf), jax.ShapeDtypeStruct((1, targets.shape[0]), f32)),
        in_specs=[hbm, vmem, vmem, hbm, hbm, hbm, hbm, hbm, hbm, hbm, vmem],
        out_specs=(vmem, vmem),
        scratch_shapes=[
            pltpu.VMEM((own * ff, depth), bf),
            pltpu.VMEM((own * ff, depth), bf),
            pltpu.VMEM(w_down.shape, bf),
            pltpu.VMEM(shared_gate.shape, bf),
            pltpu.VMEM(shared_up.shape, bf),
            pltpu.VMEM(shared_down.shape, bf),
            pltpu.VMEM(vocab.shape, bf),
            pltpu.VMEM((8, 4 * rows, cols), bf),
            pltpu.VMEM((2 * rows, own * ff), f32),
            pltpu.VMEM((2 * rows, own * ff), f32),
            pltpu.VMEM((rows, ff), f32),
            pltpu.VMEM((rows, ff), f32),
            pltpu.VMEM((8, 2 * far_rows + cap, 2 * ff), bf),
            pltpu.VMEM((own, 2 * cap, cols), f32),
            pltpu.VMEM((rows, cols), f32),
            pltpu.VMEM((4, 2, EXPERTS, rows), f32),
            pltpu.VMEM((4, rows, cols), bf),
            pltpu.VMEM((4, rows, cols), bf),
            pltpu.VMEM((4, 16, cols), bf),
            pltpu.VMEM((8, 4 * SCORE_E, cols), bf),
            pltpu.VMEM((8, 8, 128), f32),
            pltpu.VMEM((4, 8, 128), f32),
            dma((8,)),
            dma((6 * CHUNK_COPIES,)),
            dma((6 * CHUNK_COPIES,)),
            dma((24,)),
            dma((24,)),
            dma((16,)),
            dma((16,)),
        ],
        compiler_params=pltpu.CompilerParams(
            collective_id=0, has_side_effects=True, vmem_limit_bytes=60 * 2**20
        ),
    )(
        tokens, routes.T, gates.T, w_gate.reshape(own * ff, depth), w_up.reshape(own * ff, depth), w_down,
        shared_gate, shared_up, shared_down, vocab, targets.reshape(1, -1),
    )
    return out, loglik.reshape(-1)


def solution(mesh):
    placed = (
        P("expert", "tensor"),
        P("expert", None),
        P("expert", None),
        P("expert", "tensor", None),
        P("expert", "tensor", None),
        P("expert", None, "tensor"),
        P("tensor", None),
        P("tensor", None),
        P(None, "tensor"),
        P(("expert", "tensor"), None),
        P(),
    )
    fits = mesh.shape["expert"] == 4 and mesh.shape["tensor"] == 8
    return jax.shard_map(
        fused_shards if fits else shards, mesh=mesh, in_specs=placed, out_specs=(P("expert", "tensor"), P()), check_vma=False
    )
```

```python
import jax
import jax.numpy as jnp
from jax import lax
from jax.experimental import pallas as pl
from jax.experimental.pallas import tpu as pltpu
from jax.sharding import PartitionSpec as P

EXPERTS = 16
SCORE_E = 4


def slot_tables(routes, gates, capacity):
    picks = (routes[:, :, None] == jnp.arange(EXPERTS, dtype=jnp.int32)[None, None, :]).astype(
        jnp.int32
    )
    per_token = jnp.sum(picks, axis=1)
    earlier = jnp.cumsum(per_token, axis=0) - per_token
    slots = jnp.sum(picks * earlier[:, None, :], axis=2)
    places = (slots[:, :, None] == jnp.arange(capacity, dtype=jnp.int32)[None, None, :]).astype(
        jnp.float32
    )
    picked = picks.astype(jnp.float32)
    select = jnp.einsum("ikr,iks->rsi", picked, places, precision=lax.Precision.HIGHEST)
    weigh = jnp.einsum("ikr,iks,ik->rsi", picked, places, gates, precision=lax.Precision.HIGHEST)
    return (select.astype(jnp.bfloat16), weigh)


def contract_last(left, right):
    return lax.dot_general(
        left, right, (((1,), (1,)), ((), ())), preferred_element_type=jnp.float32
    )


def shards(
    tokens, routes, gates, w_gate, w_up, w_down, shared_gate, shared_up, shared_down, vocab, targets
):
    tok_rows = tokens.shape[0]
    capacity = tok_rows // 2
    groups = lax.axis_size("expert")
    lanes = lax.axis_size("tensor")
    exp_dev = w_gate.shape[0]
    width = w_gate.shape[1]
    out_width = w_down.shape[2]
    select, weigh = slot_tables(routes, gates, capacity)
    outgoing = jnp.einsum("rsi,id->rsd", select, tokens, preferred_element_type=jnp.float32).astype(
        jnp.bfloat16
    )
    arrived = lax.all_to_all(outgoing, "expert", split_axis=0, concat_axis=1, tiled=True)
    slot_count = arrived.shape[1]
    flat_rows = arrived.reshape(exp_dev * slot_count, arrived.shape[2])
    pieces = (
        lax.all_gather(flat_rows, "tensor", axis=1, tiled=True),
        lax.all_gather(tokens, "tensor", axis=1, tiled=True),
    )
    span = pieces[0].shape[1]
    rows = pieces[0].reshape(exp_dev, slot_count, span)
    gate_acc = jnp.einsum("erw,efw->erf", rows, w_gate, preferred_element_type=jnp.float32)
    up_acc = jnp.einsum("erw,efw->erf", rows, w_up, preferred_element_type=jnp.float32)
    shared_gate_acc = contract_last(pieces[1], shared_gate)
    shared_up_acc = contract_last(pieces[1], shared_up)
    hidden_routed = (jax.nn.silu(gate_acc) * up_acc).astype(jnp.bfloat16)
    hidden_shared = (jax.nn.silu(shared_gate_acc) * shared_up_acc).astype(jnp.bfloat16)
    flat_hidden = hidden_routed.reshape(exp_dev * slot_count, width)
    pieces = (
        lax.all_gather(flat_hidden, "tensor", axis=1, tiled=True),
        lax.all_gather(hidden_shared, "tensor", axis=1, tiled=True),
    )
    span = pieces[0].shape[1]
    rows = pieces[0].reshape(exp_dev, slot_count, span)
    routed_out = jnp.einsum("erw,ewd->erd", rows, w_down, preferred_element_type=jnp.float32)
    shared_out = jnp.dot(pieces[1], shared_down, preferred_element_type=jnp.float32)
    returned = lax.all_to_all(
        routed_out.astype(jnp.bfloat16), "expert", split_axis=1, concat_axis=0, tiled=True
    )
    routed = jnp.einsum(
        "rsi,rsd->id", weigh, returned.astype(jnp.float32), precision=lax.Precision.HIGHEST
    )
    layer_out = (tokens.astype(jnp.float32) + shared_out + routed).astype(jnp.bfloat16)
    scored = layer_out[tok_rows - SCORE_E :].reshape(1, SCORE_E * out_width)
    collected = lax.all_gather(scored, ("expert", "tensor"), axis=0, tiled=True)
    full_rows = (
        collected.reshape(groups, lanes, SCORE_E, out_width)
        .transpose(0, 2, 1, 3)
        .reshape(groups * SCORE_E, lanes * out_width)
    )
    logits = contract_last(full_rows, vocab)
    exp_sums = jnp.sum(jnp.exp(logits), axis=1)
    offset = (lax.axis_index("expert") * lanes + lax.axis_index("tensor")) * vocab.shape[0]
    columns = offset + jnp.arange(vocab.shape[0], dtype=jnp.int32)
    target_part = jnp.sum(jnp.where(targets[:, None] == columns[None, :], logits, 0.0), axis=1)
    totals, target_logit = lax.psum((exp_sums, target_part), ("expert", "tensor"))
    loglik = target_logit - jnp.log(totals)
    return (layer_out, loglik)


MESH_ID = pl.DeviceIdType.MESH
CHUNK_COPIES = 9
NT = (((1,), (1,)), ((), ()))


def flip(index, low):
    return index + low - 2 * low * lax.rem(lax.div(index, low), 2)


def z_peer(z, j):
    for low in (1, 2):
        if j & low:
            z = flip(z, low)
    return z


def t_peer(t, j):
    for low in (1, 2, 4):
        if j & low:
            t = flip(t, low)
    return t


def silu_mul(gate, up):
    return gate / (1.0 + jnp.exp(-gate)) * up


def layer_kernel(
    tokens, routes_t, gates_t, w_gate, w_up, w_down, shared_gate, shared_up, shared_down, vocab, targets,
    out, loglik,
    wg, wu, wd, sg, su, sd, vo, tok, acc_g, acc_u, sh_g, sh_u, hid, out_acc, sh_out, tab, part_out, part_in,
    sc, full, st_t, st_z,
    load_sem, ch_send, ch_recv, z_send, z_recv, t_send, t_recv,
):
    z, t = lax.axis_index("expert"), lax.axis_index("tensor")
    rows, cols = tokens.shape
    cap = rows // 2
    ff = sg.shape[0]

    loads = []
    pairs = (
        (tokens, tok.at[t, pl.ds(z * rows, rows)]), (shared_gate, sg), (shared_up, su), (w_gate, wg), (w_up, wu),
        (w_down, wd), (shared_down, sd), (vocab, vo),
    )
    for i, (a, b) in enumerate(pairs):
        loads.append(pltpu.make_async_copy(a, b, load_sem.at[i]))
        loads[-1].start()

    barrier = pltpu.get_barrier_semaphore()
    for j in range(1, 4):
        pl.semaphore_signal(barrier, inc=1, device_id=(z_peer(z, j), t), device_id_type=MESH_ID)
    for j in range(1, 8):
        pl.semaphore_signal(barrier, inc=1, device_id=(z, t_peer(t, j)), device_id_type=MESH_ID)

    experts = tab.shape[2]
    expert_row = lax.broadcasted_iota(jnp.int32, (experts, rows), 0)
    member = jnp.zeros((experts, rows), jnp.float32)
    weight = jnp.zeros((experts, rows), jnp.float32)
    for k in range(routes_t.shape[0]):
        hit = routes_t[k : k + 1, :] == expert_row
        member = jnp.where(hit, 1.0, member)
        weight = jnp.where(hit, gates_t[k : k + 1, :], weight)
    before = lax.broadcasted_iota(jnp.int32, (rows, rows), 0) < lax.broadcasted_iota(jnp.int32, (rows, rows), 1)
    earlier = jnp.dot(
        member.astype(jnp.bfloat16),
        jnp.where(before, 1.0, 0.0).astype(jnp.bfloat16),
        preferred_element_type=jnp.float32,
    )
    tab[0, 0] = jnp.where(member > 0.5, earlier, -1.0)
    tab[0, 1] = weight

    pl.semaphore_wait(barrier, 10)

    sends = []

    def send(src, dst, ssem, rsem, dev):
        copy = pltpu.make_async_remote_copy(
            src_ref=src, dst_ref=dst, send_sem=ssem, recv_sem=rsem, device_id=dev, device_id_type=MESH_ID
        )
        copy.start()
        sends.append(copy)

    def landed(dst, rsem):
        pltpu.make_async_remote_copy(
            src_ref=dst, dst_ref=dst, send_sem=ch_send.at[0], recv_sem=rsem, device_id=(z, t_peer(t, 1)),
            device_id_type=MESH_ID,
        ).wait_recv()

    t_c, t_x, t_y, t_d = t_peer(t, 1), t_peer(t, 2), t_peer(t, 4), t_peer(t, 6)

    class Chunk:
        def __init__(self, number, buf, start, count):
            self.base, self.buf, self.first, self.count = number * CHUNK_COPIES, buf, start, count

        def part(self, owner, which=None):
            if which is None:
                return self.buf.at[owner, pl.ds(self.first, self.count)]
            half = self.count // 2
            return self.buf.at[owner, pl.ds(self.first + which * half, half)]

        def go(self, ref, n, peer):
            send(ref, ref, ch_send.at[self.base + n], ch_recv.at[self.base + n], (z, peer))

        def got(self, ref, n):
            landed(ref, ch_recv.at[self.base + n])

        def start(self):
            for n, peer in ((0, t_x), (1, t_y), (2, t_c)):
                self.go(self.part(t), n, peer)

        def relay(self):
            self.got(self.part(t_x), 0)
            self.go(self.part(t_x, 0), 3, t_y)
            self.go(self.part(t_x), 4, t_c)
            self.got(self.part(t_y), 1)
            self.go(self.part(t_y, 1), 5, t_x)
            self.go(self.part(t_y), 6, t_c)

        def relay_far(self):
            self.got(self.part(t_d, 0), 3)
            self.go(self.part(t_d, 0), 7, t_c)
            self.got(self.part(t_d, 1), 5)
            self.go(self.part(t_d, 1), 8, t_c)

        def wait_own(self):
            self.got(self.part(t_c), 2)

        def wait_x(self):
            self.got(self.part(t_peer(t, 3)), 4)

        def wait_y(self):
            self.got(self.part(t_peer(t, 5)), 6)

        def wait_far(self):
            self.got(self.part(t_peer(t, 7), 0), 7)
            self.got(self.part(t_peer(t, 7), 1), 8)

        def finish(self):
            self.wait_own()
            self.wait_x()
            self.wait_y()
            self.wait_far()

    groups = [z, z_peer(z, 1), z_peer(z, 2), z_peer(z, 3)]
    chunks = [Chunk(k, tok, groups[k] * rows, rows) for k in range(4)]
    far_rows, own_rows = 8 * cap // 2, 8 * cap // 2 + cap
    hid_far = Chunk(4, hid, 0, far_rows)
    hid_own = Chunk(5, hid, far_rows, own_rows)
    loads[0].wait()
    for j in (1, 2, 3):
        mine = tok.at[t, pl.ds(z * rows, rows)]
        send(mine, mine, z_send.at[j], z_recv.at[j], (groups[j], t))
    for j in (1, 2, 3):
        send(tab.at[0], tab.at[j], z_send.at[4 + j], z_recv.at[4 + j], (groups[j], t))
    chunks[0].start()

    def z_landed(j):
        landed(chunks[j].part(t), z_recv.at[j])
        chunks[j].start()

    z_landed(1)
    chunks[0].relay()
    z_landed(2)
    chunks[1].relay()
    chunks[0].relay_far()
    z_landed(3)
    for load in loads[1:5]:
        load.wait()
    chunks[1].relay_far()
    chunks[0].finish()
    chunks[1].finish()

    def clear():
        acc_g[...] = jnp.zeros_like(acc_g)
        acc_u[...] = jnp.zeros_like(acc_u)

    def up_seg(pair, chip, shared):
        def step(i, carry):
            owner = 2 * chip + i
            span = pl.ds(pl.multiple_of(owner * cols, 128), cols)
            x = tok[owner, pl.ds(pl.multiple_of(pair * 2 * rows, 128), 2 * rows), :]
            acc_g[...] += lax.dot_general(x, wg[:, span], NT, preferred_element_type=jnp.float32)
            acc_u[...] += lax.dot_general(x, wu[:, span], NT, preferred_element_type=jnp.float32)
            if shared:
                own = tok[owner, pl.ds(pl.multiple_of(z * rows, 128), rows), :]
                sh_g[...] += lax.dot_general(own, sg[:, span], NT, preferred_element_type=jnp.float32)
                sh_u[...] += lax.dot_general(own, su[:, span], NT, preferred_element_type=jnp.float32)
            return carry

        lax.fori_loop(0, 2, step, 0)

    slot_no = lax.broadcasted_iota(jnp.int32, (cap, rows), 0).astype(jnp.float32)

    def table_of(j):
        first = pl.ds(4 * z, 4)
        return tab[j, 0, first, :], tab[j, 1, first, :]

    def squeeze(first_row, js):
        for j in js:
            place = lax.rem(groups[j], 2)
            span = pl.ds(pl.multiple_of(place * rows, 128), rows)
            h = silu_mul(acc_g[span, :], acc_u[span, :]).astype(jnp.bfloat16)
            slots, _ = table_of(j)
            for q in range(2):
                both = h[:, 2 * q * ff : 2 * (q + 1) * ff]
                picked = []
                for e in (2 * q, 2 * q + 1):
                    sel = jnp.where(slot_no == slots[e : e + 1, :], 1.0, 0.0).astype(jnp.bfloat16)
                    picked.append(jnp.dot(sel, both, preferred_element_type=jnp.float32))
                lane = lax.broadcasted_iota(jnp.int32, picked[0].shape, 1)
                at = pl.ds(pl.multiple_of(first_row + q * 2 * cap + place * cap, 16), cap)
                hid[t, at, :] = jnp.where(lane < ff, picked[0], picked[1]).astype(jnp.bfloat16)

    chip, chip_x, chip_y, chip_d = [lax.div(v, 2) for v in (t, t_x, t_y, t_d)]
    own_pair, far_pair = lax.div(z, 2), 1 - lax.div(z, 2)
    clear()
    sh_g[...] = jnp.zeros_like(sh_g)
    sh_u[...] = jnp.zeros_like(sh_u)
    up_seg(own_pair, chip, True)
    chunks[2].relay()
    up_seg(own_pair, chip_x, True)
    up_seg(own_pair, chip_y, True)
    chunks[3].relay()
    chunks[2].relay_far()
    up_seg(own_pair, chip_d, True)
    for j in (1, 2, 3):
        landed(tab.at[j], z_recv.at[4 + j])
    squeeze(far_rows, (0, 1))
    hs = silu_mul(sh_g[...], sh_u[...])
    hid[t, pl.ds(2 * far_rows, cap), :] = jnp.concatenate([hs[:cap], hs[cap:]], axis=1).astype(jnp.bfloat16)
    hid_own.start()
    clear()
    chunks[3].relay_far()
    for c in (2, 3):
        chunks[c].wait_own()
    up_seg(far_pair, chip, False)
    for c in (2, 3):
        chunks[c].wait_x()
    up_seg(far_pair, chip_x, False)
    for c in (2, 3):
        chunks[c].wait_y()
    up_seg(far_pair, chip_y, False)
    hid_own.relay()
    for c in (2, 3):
        chunks[c].wait_far()
    up_seg(far_pair, chip_d, False)
    squeeze(0, (2, 3))
    hid_far.start()
    hid_own.relay_far()
    for load in loads[5:]:
        load.wait()

    def down_seg(first_row, chip_no, shared):
        def step(i, carry):
            owner = 2 * chip_no + i
            span = pl.ds(pl.multiple_of(owner * ff, 16), ff)
            for q in range(2):
                h = hid[owner, pl.ds(first_row + q * 2 * cap, 2 * cap), :]
                for k in range(2):
                    out_acc[2 * q + k] += jnp.dot(
                        h[:, k * ff : (k + 1) * ff], wd[2 * q + k, span, :], preferred_element_type=jnp.float32
                    )
            if shared:
                h = hid[owner, pl.ds(2 * far_rows, cap), :]
                for k in range(2):
                    sh_out[k * cap : (k + 1) * cap, :] += jnp.dot(
                        h[:, k * ff : (k + 1) * ff], sd[span, :], preferred_element_type=jnp.float32
                    )
            return carry

        lax.fori_loop(0, 2, step, 0)

    def combine(j):
        place = lax.rem(groups[j], 2)
        span = pl.ds(pl.multiple_of(place * cap, 16), cap)
        slots, weights = table_of(j)
        ys = jnp.concatenate([out_acc[e, span, :].astype(jnp.bfloat16) for e in range(4)], axis=0)
        mix = jnp.concatenate(
            [jnp.where(slot_no == slots[e : e + 1, :], weights[e : e + 1, :], 0.0) for e in range(4)], axis=0
        ).T
        high = mix.astype(jnp.bfloat16)
        low = (mix - high.astype(jnp.float32)).astype(jnp.bfloat16)
        return jnp.dot(high, ys, preferred_element_type=jnp.float32) + jnp.dot(
            low, ys, preferred_element_type=jnp.float32
        )

    def give(j):
        part_out[j] = combine(j).astype(jnp.bfloat16)
        send(part_out.at[j], part_in.at[j], z_send.at[8 + j], z_recv.at[8 + j], (groups[j], t))

    out_acc[...] = jnp.zeros_like(out_acc)
    sh_out[...] = jnp.zeros_like(sh_out)
    hid_far.wait_own()
    down_seg(0, chip, False)
    hid_far.relay()
    hid_far.wait_x()
    down_seg(0, chip_x, False)
    hid_far.relay_far()
    hid_far.wait_y()
    down_seg(0, chip_y, False)
    hid_far.wait_far()
    down_seg(0, chip_d, False)
    give(2)
    give(3)
    out_acc[...] = jnp.zeros_like(out_acc)
    hid_own.wait_own()
    down_seg(far_rows, chip, True)
    hid_own.wait_x()
    down_seg(far_rows, chip_x, True)
    hid_own.wait_y()
    down_seg(far_rows, chip_y, True)
    hid_own.wait_far()
    down_seg(far_rows, chip_d, True)
    give(1)
    total = tok[t, pl.ds(pl.multiple_of(z * rows, 128), rows), :].astype(jnp.float32) + sh_out[...] + combine(0)
    for j in (1, 2, 3):
        landed(part_in.at[j], z_recv.at[8 + j])
        total += part_in[j].astype(jnp.float32)
    layer = total.astype(jnp.bfloat16)
    out[...] = layer

    sc[z] = layer[rows - 16 :, :]
    for j in (1, 2, 3):
        send(sc.at[z], sc.at[z], z_send.at[12 + j], z_recv.at[12 + j], (groups[j], t))
    for j in (1, 2, 3):
        landed(sc.at[groups[j]], z_recv.at[12 + j])
    full[t] = jnp.concatenate(
        [sc[g].astype(jnp.float32)[16 - SCORE_E :, :] for g in range(4)], axis=0
    ).astype(jnp.bfloat16)
    for j in range(1, 8):
        send(full.at[t], full.at[t], t_send.at[j], t_recv.at[j], (z, t_peer(t, j)))
    logits = jnp.zeros((vo.shape[0], full.shape[1]), jnp.float32)
    for j in range(8):
        owner = t_peer(t, j)
        if j:
            landed(full.at[owner], t_recv.at[j])
        span = pl.ds(pl.multiple_of(owner * cols, 128), cols)
        logits += lax.dot_general(vo[:, span], full[owner], NT, preferred_element_type=jnp.float32)
    offset = (z * 8 + t) * vo.shape[0]
    entry = offset + lax.broadcasted_iota(jnp.int32, logits.shape, 0)
    st_t[0] = jnp.zeros_like(st_t[0])
    st_t[0, 0:1, 0:16] = jnp.sum(jnp.exp(logits), axis=0, keepdims=True)
    st_t[0, 1:2, 0:16] = jnp.sum(jnp.where(entry == targets[...], logits, 0.0), axis=0, keepdims=True)
    for j in range(1, 8):
        send(st_t.at[0], st_t.at[j], t_send.at[8 + j], t_recv.at[8 + j], (z, t_peer(t, j)))
    summed = st_t[0]
    for j in range(1, 8):
        landed(st_t.at[j], t_recv.at[8 + j])
        summed += st_t[j]
    st_z[z] = summed
    for j in (1, 2, 3):
        send(st_z.at[z], st_z.at[z], z_send.at[16 + j], z_recv.at[16 + j], (groups[j], t))
    for j in (1, 2, 3):
        landed(st_z.at[groups[j]], z_recv.at[16 + j])
    both = ((st_z[0] + st_z[1]) + st_z[2]) + st_z[3]
    loglik[...] = both[1:2, 0:16] - jnp.log(both[0:1, 0:16])
    for copy in sends:
        copy.wait_send()


def fused_shards(
    tokens, routes, gates, w_gate, w_up, w_down, shared_gate, shared_up, shared_down, vocab, targets
):
    rows, cols = tokens.shape
    own, ff, depth = w_gate.shape
    cap = rows // 2
    far_rows = 4 * cap
    bf, f32 = jnp.bfloat16, jnp.float32
    hbm, vmem = pl.BlockSpec(memory_space=pl.ANY), pl.BlockSpec(memory_space=pltpu.VMEM)
    dma = pltpu.SemaphoreType.DMA
    out, loglik = pl.pallas_call(
        layer_kernel,
        out_shape=(jax.ShapeDtypeStruct((rows, cols), bf), jax.ShapeDtypeStruct((1, targets.shape[0]), f32)),
        in_specs=[hbm, vmem, vmem, hbm, hbm, hbm, hbm, hbm, hbm, hbm, vmem],
        out_specs=(vmem, vmem),
        scratch_shapes=[
            pltpu.VMEM((own * ff, depth), bf),
            pltpu.VMEM((own * ff, depth), bf),
            pltpu.VMEM(w_down.shape, bf),
            pltpu.VMEM(shared_gate.shape, bf),
            pltpu.VMEM(shared_up.shape, bf),
            pltpu.VMEM(shared_down.shape, bf),
            pltpu.VMEM(vocab.shape, bf),
            pltpu.VMEM((8, 4 * rows, cols), bf),
            pltpu.VMEM((2 * rows, own * ff), f32),
            pltpu.VMEM((2 * rows, own * ff), f32),
            pltpu.VMEM((rows, ff), f32),
            pltpu.VMEM((rows, ff), f32),
            pltpu.VMEM((8, 2 * far_rows + cap, 2 * ff), bf),
            pltpu.VMEM((own, 2 * cap, cols), f32),
            pltpu.VMEM((rows, cols), f32),
            pltpu.VMEM((4, 2, EXPERTS, rows), f32),
            pltpu.VMEM((4, rows, cols), bf),
            pltpu.VMEM((4, rows, cols), bf),
            pltpu.VMEM((4, 16, cols), bf),
            pltpu.VMEM((8, 4 * SCORE_E, cols), bf),
            pltpu.VMEM((8, 8, 128), f32),
            pltpu.VMEM((4, 8, 128), f32),
            dma((8,)),
            dma((6 * CHUNK_COPIES,)),
            dma((6 * CHUNK_COPIES,)),
            dma((20,)),
            dma((20,)),
            dma((16,)),
            dma((16,)),
        ],
        compiler_params=pltpu.CompilerParams(
            collective_id=0, has_side_effects=True, vmem_limit_bytes=60 * 2**20
        ),
    )(
        tokens, routes.T, gates.T, w_gate.reshape(own * ff, depth), w_up.reshape(own * ff, depth), w_down,
        shared_gate, shared_up, shared_down, vocab, targets.reshape(1, -1),
    )
    return out, loglik.reshape(-1)


def solution(mesh):
    placed = (
        P("expert", "tensor"),
        P("expert", None),
        P("expert", None),
        P("expert", "tensor", None),
        P("expert", "tensor", None),
        P("expert", None, "tensor"),
        P("tensor", None),
        P("tensor", None),
        P(None, "tensor"),
        P(("expert", "tensor"), None),
        P(),
    )
    fits = mesh.shape["expert"] == 4 and mesh.shape["tensor"] == 8
    return jax.shard_map(
        fused_shards if fits else shards, mesh=mesh, in_specs=placed, out_specs=(P("expert", "tensor"), P()), check_vma=False
    )
```
